32 devices in a mesh: parts: 1, ep: 32 (over z, y, x, core), ex: 1.
Axes of the slice: x: 2, y: 2, z: 4, core: 2. Of those that a mesh axis runs over, the one named last changes fastest.
Arguments:
- residual: bfloat16 [256, 4096], P(('parts', 'ep', 'ex')), may hold values from -6 to 6
- queries: bfloat16 [256, 4096], P(('parts', 'ep', 'ex')), may hold values from -80 to 80
- new_kv: bfloat16 [256, 512], P(('parts', 'ep', 'ex')), may hold values from -4 to 4
- cache_pool: bfloat16 [2048, 16, 512], P(('parts', 'ep', 'ex')), may hold values from -6 to 6
- page_table: int32 [32, 64], P(('parts', 'ep', 'ex')), may hold values from 0 to 63, each once within a row
- context_len: int32 [32, 8], P(('parts', 'ep', 'ex')), may hold values from 1 to 128, 576 in all within a row
- prefill_hidden: bfloat16 [1792, 4096], P(('parts', 'ep', 'ex')), may hold values from -6 to 6
- prefill_kv: bfloat16 [1792, 512], P(('parts', 'ep', 'ex')), may hold values from -6 to 6
- prefill_dest: int32 [1792, 1], P(('parts', 'ep', 'ex')), may hold values from 0 to 31; in each aligned block of 56 rows (0 to 55, 56 to 111, ...) at most 3 rows name the same one
- prefill_slot: int32 [1792], P(('parts', 'ep', 'ex')), may hold values from 0 to 7
- expert_ids: int32 [2048, 8], P(('parts', 'ep', 'ex')), may hold values from 0 to 31, all different within a row; in each aligned block of 64 rows (0 to 63, 64 to 127, ...) at most 20 rows name the same one
- gate_values: float32 [2048, 8], P(('parts', 'ep', 'ex')), may hold values from 0.05 to 0.3
- norm_gain: float32 [4096], replicated, may hold values from 0.5 to 1.5
- gate_weight: bfloat16 [32, 4096, 768], P('ep', None, 'ex'), may hold values from -0.09375 to 0.09375
- up_weight: bfloat16 [32, 4096, 768], P('ep', None, 'ex'), may hold values from -0.09375 to 0.09375
- down_weight: bfloat16 [32, 768, 4096], P('ep', 'ex'), may hold values from -0.21875 to 0.21875
Outputs:
- decode_out: bfloat16 [256, 4096], P(('parts', 'ep', 'ex'))
- prefill_out: bfloat16 [1792, 4096], P(('parts', 'ep', 'ex'))
The draws below stay inside these ranges and needn't reach their ends.
Inputs may be any that keep to these rules, and one draw needn't show every extreme that they name: `page_table`: each row is a permutation of one device's 64 local pages; request i of that device reads entries i * 8 to (i + 1) * 8 - 1 in order. `context_len`: each device's lengths sum to 576 and one of them is 128. `prefill_dest`: device index in ep+ex order inside the group; at most 3 of one device's prefill tokens name one device, and that many do on some device. `expert_ids`: the experts of a row differ; at most 20 of one device's 64 rows name one expert, and that many do on some device.
All inputs are finite; a program needn't handle non-finite values.
Results may differ from the reference program's by a relative error of at most 0.007.
Values may be sent and summed in bfloat16 or wider, within the bound.
A program may use at most 128 MiB of HBM per device.

```python
import math
import jax
import jax.numpy as jnp
import numpy as np
from jax import lax

D = 4096
HD = 128
TOP = 8
KVH = 2
HID = 768
DEC_DEV = 8
PRE_DEV = 56
CTX = 128
PAGE = 16
DEVS = 32
KV_CAP = 3
EXPERTS = 32
ROW_DEV = 64
CAP = 20
PAGES_REQ = 8
POOL_DEV = 64
DEC_TOKENS = 256
PRE_TOKENS = 1792
ROWS = 2048
N_EP = 32
N_EX = 1


def common_keys(key):
    return jnp.clip(jax.random.normal(key, (DEC_TOKENS, KVH * HD), jnp.float32), -4.0, 4.0)


def draw_new_kv(key, part):
    shared = common_keys(key)
    key = jax.random.fold_in(key, 5)
    values = jnp.clip(jax.random.normal(key, (DEC_TOKENS, KVH * HD), jnp.float32), -4.0, 4.0)
    return jnp.concatenate([shared, values], axis=1).astype(jnp.bfloat16)


def draw_queries(key, part):
    key = jax.random.fold_in(key, 9)
    key_values = jax.random.fold_in(key, 0)
    query_vals = jnp.clip(jax.random.normal(key_values, (DEC_TOKENS, D), jnp.float32), -6.0, 6.0)
    return query_vals.astype(jnp.bfloat16)


def plant(drawn, rng, least, top_value):
    dims = drawn.shape
    place = [jax.random.randint(jax.random.fold_in(rng, axis), (), 0, dims[axis]) for axis in range(len(dims))]
    drawn = drawn.at[tuple(place)].set(least)
    longest = dims.index(max(dims))
    place[longest] = (place[longest] + 1) % dims[longest]
    return drawn.at[tuple(place)].set(top_value)


def block_scale(own_key, dims, shards, least, high):
    factor_of = 1.0
    for axis_at, shards_of in shards:
        heights = jax.random.uniform(jax.random.fold_in(jax.random.fold_in(own_key, 6), axis_at), (shards_of,), jnp.float32, least / len(shards), high / len(shards))
        factor_of = factor_of * jnp.repeat(jnp.exp(heights), dims[axis_at] // shards_of).reshape((-1,) + (1,) * (len(dims) - 1 - axis_at))
    return factor_of


def profile(count, total, bound, slope):
    loads = [(1 << 20) // math.isqrt(rank ** slope) + 1 for rank in range(2, count + 1)]
    spare, given = total - bound - (count - 1), [1] * (count - 1)
    while spare > 0:
        movable = [i for i in range(count - 1) if given[i] < bound]
        whole, budget = sum([loads[i] for i in movable]), spare
        for i in movable:
            extra = min(bound - given[i], max(1, budget * loads[i] // whole), spare)
            given[i] = given[i] + extra
            spare = spare - extra
    return np.array([bound] + given)


def uneven_parts(stream_key, count, total, most, slope):
    if count == 2:
        one = jax.random.randint(stream_key, (), max(1, total - most), min(most, total - 1) + 1)
        return jnp.stack([one, total - one])
    lengths = jnp.asarray(profile(count, total, most, slope), jnp.int32)
    couples = (count - 1) // 2
    giver, sink = lengths[1:1 + 2 * couples:2], lengths[2:2 + 2 * couples:2]
    margin = jnp.minimum(giver - 1, most - sink)
    shifted = jax.random.randint(jax.random.fold_in(stream_key, 1), (couples,), 0, 1 << 20) % (margin + 1)
    lengths = lengths.at[1:1 + 2 * couples:2].set(giver - shifted).at[2:2 + 2 * couples:2].set(sink + shifted)
    return lengths[jax.random.permutation(jax.random.fold_in(stream_key, 2), count)]


def routed_block(key, own, number, rows, amount, top, reach, lean):
    sequence = jax.random.permutation(key, amount)
    heavy_load, usual = shares(amount, rows * top, reach, lean, True), shares(amount, rows * top, reach, lean, False)
    places = jnp.arange(amount)

    def named(lengths, rotation):
        used = int((lengths > 0).sum())
        fixed = max(1, used // 4)
        shifted = fixed + (places - fixed + rotation * (used - fixed)) % max(1, amount - fixed)
        return jnp.zeros((amount,), jnp.int32).at[sequence[jnp.where(places < fixed, places, shifted)]].set(jnp.asarray(lengths, jnp.int32))

    lengths = jnp.where(number % 4 == 0, named(heavy_load, number // 4), named(usual, number - number // 4 - 1))
    mixed = jax.random.permutation(jax.random.fold_in(own, 3), amount)
    donor, sink = mixed[0:amount // 2 * 2:2], mixed[1:amount // 2 * 2:2]
    room = jnp.minimum(lengths[donor] - 1, reach - lengths[sink]) // 2
    room = jnp.where((donor == sequence[0]) | (sink == sequence[0]) | (lengths[sink] == 0), 0, jnp.maximum(room, 0))
    shifted = jax.random.randint(jax.random.fold_in(own, 4), (amount // 2,), 0, 1 << 20) % (room + 1)
    lengths = lengths.at[donor].add(-shifted).at[sink].add(shifted)
    items = jnp.searchsorted(jnp.cumsum(lengths), jnp.arange(rows * top), side="right").astype(jnp.int32)
    listing = items.reshape(top, rows).T
    listing = listing[jax.random.permutation(jax.random.fold_in(own, 1), rows)]
    rotation = jax.random.randint(jax.random.fold_in(own, 2), (rows, 1), 0, top)
    return jnp.take_along_axis(listing, (jnp.arange(top)[None, :] + rotation) % top, axis=1)


def shares(amount, total, most, skew, full):
    portions = [(1 << 20) // math.isqrt(standing ** skew) + 1 for standing in range(1, amount + 1)]
    largest = most if full else min(most, max(-(-total // amount), total * portions[0] // sum(portions)))
    least = 1 if total - largest >= amount - 1 else 0
    holding, surplus = [largest] + [least] * (amount - 1), total - largest - least * (amount - 1)
    while surplus > 0:
        candidates = [i for i in range(1, amount) if holding[i] < largest] or [i for i in range(1, amount) if holding[i] < most]
        pool, remaining = sum([portions[i] for i in candidates]), surplus
        for i in candidates:
            extra = min(most - holding[i], max(1, remaining * portions[i] // pool), surplus)
            holding[i] = holding[i] + extra
            surplus = surplus - extra
    return np.array(holding)


def bell_draw(key, dims, spread, most, pieces=(), held_as=jnp.bfloat16):
    level = block_scale(key, dims, pieces, -0.22, 0.18) if pieces else 1.0
    values = jax.random.normal(key, dims, jnp.float32) * spread * level
    return jnp.minimum(jnp.maximum(values, -most), most).astype(held_as)


def setup_inputs(seed: int = 0, part: int = 0) -> dict:
    key_of = jax.random.split(jax.random.key(seed), 17)
    part_keys = jax.random.split(jax.random.fold_in(key_of[16], part), 17)
    residual = bell_draw(part_keys[0], (DEC_TOKENS, D), 1.0, 6.0, ((0, 32),))
    queries = draw_queries(jax.random.fold_in(jax.random.fold_in(key_of[16], part), 71), part)
    new_kv = draw_new_kv(jax.random.fold_in(jax.random.fold_in(key_of[16], part), 71), part)
    cache_pool = bell_draw(part_keys[3], (DEVS * POOL_DEV, PAGE, 2 * KVH * HD), 1.0, 6.0, ((0, 32),))
    page_table = jax.vmap(lambda own: jax.random.permutation(own, POOL_DEV))(jax.random.split(part_keys[4], DEVS)).reshape((DEVS, POOL_DEV)).astype(jnp.int32)
    context_len = jax.vmap(lambda own: uneven_parts(own, DEC_DEV, (DEC_DEV * CTX + CTX) // 2, CTX, 2))(jax.random.split(part_keys[5], DEVS)).reshape((DEVS, DEC_DEV)).astype(jnp.int32)
    prefill_hidden = bell_draw(part_keys[6], (PRE_TOKENS, D), 1.0, 6.0, ((0, 32),))
    prefill_kv = bell_draw(part_keys[7], (PRE_TOKENS, 2 * KVH * HD), 1.0, 6.0, ((0, 32),))
    prefill_dest_keys = jax.random.split(jax.random.fold_in(part_keys[8], 1), PRE_TOKENS // PRE_DEV)
    prefill_dest_turns = jax.random.permutation(jax.random.fold_in(part_keys[8], 3), PRE_TOKENS // PRE_DEV)
    prefill_dest = jax.vmap(lambda own, number: routed_block(jax.random.fold_in(part_keys[8], 2), own, number, PRE_DEV, DEVS, 1, KV_CAP, 2))(prefill_dest_keys, prefill_dest_turns).reshape((PRE_TOKENS, 1))
    prefill_slot = plant(jax.random.randint(part_keys[9], (PRE_TOKENS,), 0, DEC_DEV), jax.random.fold_in(part_keys[9], 1), 0, DEC_DEV - 1).astype(jnp.int32)
    expert_ids_keys = jax.random.split(jax.random.fold_in(part_keys[10], 1), ROWS // ROW_DEV)
    expert_ids_turns = jax.random.permutation(jax.random.fold_in(part_keys[10], 3), ROWS // ROW_DEV)
    expert_ids = jax.vmap(lambda own, number: routed_block(jax.random.fold_in(part_keys[10], 2), own, number, ROW_DEV, EXPERTS, TOP, CAP, 2))(expert_ids_keys, expert_ids_turns).reshape((ROWS, TOP))
    gate_values = jnp.clip(0.05 + 0.25 * jax.random.uniform(part_keys[11], (ROWS, TOP), jnp.float32) ** block_scale(part_keys[11], (ROWS, TOP), ((0, 32),), -0.2, 0.2), 0.05, 0.3)
    norm_gain = jnp.clip(1.0 + 0.1 * jax.random.normal(key_of[12], (D,), jnp.float32), 0.5, 1.5)
    gate_weight = bell_draw(key_of[13], (EXPERTS, D, HID), D ** -0.5, 0.09375, ((0, 32),))
    up_weight = bell_draw(key_of[14], (EXPERTS, D, HID), D ** -0.5, 0.09375, ((0, 32),))
    down_weight = bell_draw(key_of[15], (EXPERTS, HID, D), HID ** -0.5, 0.21875, ((0, 32),))
    return {"residual": residual, "queries": queries, "new_kv": new_kv, "cache_pool": cache_pool, "page_table": page_table, "context_len": context_len, "prefill_hidden": prefill_hidden, "prefill_kv": prefill_kv, "prefill_dest": prefill_dest, "prefill_slot": prefill_slot, "expert_ids": expert_ids, "gate_values": gate_values, "norm_gain": norm_gain, "gate_weight": gate_weight, "up_weight": up_weight, "down_weight": down_weight}


neg_big = -1e+30
eps = 1e-06

def attend(queries, new_kv, cache, context_len, hand_kv, hand_ok):
    row_count = queries.shape[0]
    kv_width = new_kv.shape[1] // 2
    group_size = queries.shape[1] // kv_width
    positions = cache.shape[1]
    query_heads = queries.astype(jnp.float32).reshape(row_count, KVH, group_size, HD)
    cache_keys = cache[:, :, :kv_width].astype(jnp.float32).reshape(row_count, positions, KVH, HD)
    cache_values = cache[:, :, kv_width:].astype(jnp.float32).reshape(row_count, positions, KVH, HD)
    hand_keys = hand_kv[:, :kv_width].astype(jnp.float32).reshape(-1, KVH, HD)
    hand_values = hand_kv[:, kv_width:].astype(jnp.float32).reshape(-1, KVH, HD)
    own_keys = new_kv[:, :kv_width].astype(jnp.float32).reshape(row_count, KVH, HD)
    own_values = new_kv[:, kv_width:].astype(jnp.float32).reshape(row_count, KVH, HD)
    score_scale = HD ** (-0.5)
    cache_scores = jnp.einsum('rgjd,rtgd->rgjt', query_heads, cache_keys) * score_scale
    live_mask = jnp.arange(positions, dtype=jnp.int32)[None, :] < context_len[:, None]
    cache_scores = jnp.where(live_mask[:, None, None, :], cache_scores, neg_big)
    hand_scores = jnp.einsum('rgjd,mgd->rgjm', query_heads, hand_keys) * score_scale
    hand_scores = jnp.where(hand_ok[:, None, None, :], hand_scores, neg_big)
    own_scores = jnp.einsum('rgjd,rgd->rgj', query_heads, own_keys) * score_scale
    largest = jnp.maximum(jnp.maximum(lax.optimization_barrier(jnp.max(cache_scores, -1)), lax.optimization_barrier(jnp.max(hand_scores, -1))), own_scores)
    cache_exp = jnp.exp(cache_scores - largest[..., None])
    hand_exp = jnp.exp(hand_scores - largest[..., None])
    own_exp = jnp.exp(own_scores - largest)
    denominator = lax.optimization_barrier(jnp.sum(cache_exp, -1)) + lax.optimization_barrier(jnp.sum(hand_exp, -1)) + own_exp
    cache_probs = (cache_exp / denominator[..., None]).astype(jnp.bfloat16).astype(jnp.float32)
    hand_probs = (hand_exp / denominator[..., None]).astype(jnp.bfloat16).astype(jnp.float32)
    own_probs = (own_exp / denominator).astype(jnp.bfloat16).astype(jnp.float32)
    attended = jnp.einsum('rgjt,rtgd->rgjd', cache_probs, cache_values)
    attended = attended + jnp.einsum('rgjm,mgd->rgjd', hand_probs, hand_values)
    attended = attended + own_probs[..., None] * own_values[:, :, None, :]
    return attended.reshape(row_count, -1)

def expert_out(rows_in, gate_mat, up_mat, down_mat):
    gate_act = jnp.dot(rows_in, gate_mat, preferred_element_type=jnp.float32)
    up_act = jnp.dot(rows_in, up_mat, preferred_element_type=jnp.float32)
    hidden = (jax.nn.silu(gate_act) * up_act).astype(jnp.bfloat16)
    block_size = hidden.shape[1] // N_EX
    summed = jnp.zeros((rows_in.shape[0], down_mat.shape[1]), jnp.float32)
    for half_index in range(N_EX):
        low = half_index * block_size
        block_term = jnp.dot(hidden[:, low:low + block_size], down_mat[low:low + block_size], preferred_element_type=jnp.float32).astype(jnp.bfloat16)
        summed = summed + lax.optimization_barrier(block_term).astype(jnp.float32)
    return summed.astype(jnp.bfloat16)

def reference(residual, queries, new_kv, cache_pool, page_table, context_len, prefill_hidden, prefill_kv, prefill_dest, prefill_slot, expert_ids, gate_values, norm_gain, gate_weight, up_weight, down_weight):
    device_count = N_EP * N_EX
    pool_blocks = cache_pool.reshape(device_count, POOL_DEV, PAGE, -1)
    targets = prefill_dest[:, 0]

    def per_device(device):
        pages = page_table[device].reshape(DEC_DEV, PAGES_REQ)
        cache = pool_blocks[device][pages].reshape(DEC_DEV, CTX, -1)
        first_row = device * DEC_DEV
        query_rows = lax.dynamic_slice_in_dim(queries, first_row, DEC_DEV, 0)
        own_rows = lax.dynamic_slice_in_dim(new_kv, first_row, DEC_DEV, 0)
        hand_ok = (targets[None, :] == device) & (prefill_slot[None, :] == jnp.arange(DEC_DEV, dtype=jnp.int32)[:, None])
        return attend(query_rows, own_rows, cache, context_len[device], prefill_kv, hand_ok)
    attention = lax.map(per_device, jnp.arange(device_count, dtype=jnp.int32)).reshape(DEC_TOKENS, D)
    decode_sum = residual.astype(jnp.float32) + attention
    residual_sum = jnp.concatenate([decode_sum.reshape(device_count, DEC_DEV, D), prefill_hidden.astype(jnp.float32).reshape(device_count, PRE_DEV, D)], axis=1).reshape(ROWS, D)
    mean_square = lax.optimization_barrier(jnp.mean(residual_sum * residual_sum, axis=1, keepdims=True))
    normed = (residual_sum * lax.rsqrt(mean_square + eps) * norm_gain).astype(jnp.bfloat16)
    limit = device_count * CAP

    def per_expert(running, expert):
        hit_mask = expert_ids == expert
        routed = jnp.any(hit_mask, axis=1)
        row_weight = lax.optimization_barrier(jnp.sum(jnp.where(hit_mask, gate_values, jnp.zeros_like(gate_values)), axis=1))
        order = jnp.cumsum(routed.astype(jnp.int32)) - 1
        target_spot = jnp.where(routed, order, limit)
        picked_rows = jnp.zeros((limit,), jnp.int32).at[target_spot].set(jnp.arange(ROWS, dtype=jnp.int32), mode='drop')
        valid = jnp.arange(limit, dtype=jnp.int32) < jnp.sum(routed.astype(jnp.int32))
        outputs = expert_out(normed[picked_rows], gate_weight[expert], up_weight[expert], down_weight[expert])
        contrib = jnp.where(valid[:, None], row_weight[picked_rows][:, None] * outputs.astype(jnp.float32), jnp.zeros((), jnp.float32))
        return (running.at[picked_rows].add(contrib), None)
    mixture, unused = lax.scan(per_expert, jnp.zeros((ROWS, D), jnp.float32), jnp.arange(EXPERTS, dtype=jnp.int32))
    result = (residual_sum + mixture).astype(jnp.bfloat16).reshape(device_count, ROW_DEV, D)
    return (result[:, :DEC_DEV].reshape(DEC_TOKENS, D), result[:, DEC_DEV:].reshape(PRE_TOKENS, D))
```

```python
import functools

import jax
import jax.numpy as jnp
from jax import lax
from jax.experimental import pallas as pl
from jax.experimental.pallas import tpu as pltpu
from jax.sharding import PartitionSpec as P

HD = 128
KVH = 2


neg_big = -1e30
eps = 1e-06


def attend(queries, new_kv, cache, context_len, hand_kv, hand_ok):
    row_count = queries.shape[0]
    kv_width = new_kv.shape[1] // 2
    group_size = queries.shape[1] // kv_width
    positions = cache.shape[1]
    query_heads = queries.reshape(row_count, KVH, group_size, HD)
    cache_keys = cache[:, :, :kv_width].reshape(row_count, positions, KVH, HD)
    cache_values = cache[:, :, kv_width:].reshape(row_count, positions, KVH, HD)
    hand_keys = hand_kv[:, :kv_width].reshape(-1, KVH, HD)
    hand_values = hand_kv[:, kv_width:].reshape(-1, KVH, HD)
    own_keys = new_kv[:, :kv_width].reshape(row_count, KVH, HD)
    own_values = new_kv[:, kv_width:].reshape(row_count, KVH, HD)
    score_scale = HD ** (-0.5)
    cache_scores = (
        jnp.einsum("rgjd,rtgd->rgjt", query_heads, cache_keys, preferred_element_type=jnp.float32)
        * score_scale
    )
    live_mask = jnp.arange(positions, dtype=jnp.int32)[None, :] < context_len[:, None]
    cache_scores = jnp.where(live_mask[:, None, None, :], cache_scores, neg_big)
    hand_scores = (
        jnp.einsum("rgjd,mgd->rgjm", query_heads, hand_keys, preferred_element_type=jnp.float32)
        * score_scale
    )
    hand_scores = jnp.where(hand_ok[:, None, None, :], hand_scores, neg_big)
    own_scores = (
        jnp.einsum("rgjd,rgd->rgj", query_heads, own_keys, preferred_element_type=jnp.float32)
        * score_scale
    )
    largest = jnp.maximum(
        jnp.maximum(jnp.max(cache_scores, -1), jnp.max(hand_scores, -1)), own_scores
    )
    cache_exp = jnp.exp(cache_scores - largest[..., None])
    hand_exp = jnp.exp(hand_scores - largest[..., None])
    own_exp = jnp.exp(own_scores - largest)
    denominator = jnp.sum(cache_exp, -1) + jnp.sum(hand_exp, -1) + own_exp
    cache_probs = (cache_exp / denominator[..., None]).astype(jnp.bfloat16)
    hand_probs = (hand_exp / denominator[..., None]).astype(jnp.bfloat16)
    own_probs = (own_exp / denominator).astype(jnp.bfloat16)
    attended = jnp.einsum(
        "rgjt,rtgd->rgjd", cache_probs, cache_values, preferred_element_type=jnp.float32
    )
    attended = attended + jnp.einsum(
        "rgjm,mgd->rgjd", hand_probs, hand_values, preferred_element_type=jnp.float32
    )
    attended = (
        attended
        + own_probs.astype(jnp.float32)[..., None] * own_values.astype(jnp.float32)[:, :, None, :]
    )
    return attended.reshape(row_count, -1)


def expert_terms(slot_rows, gate_weight, up_weight, down_weight):
    gate_act = jnp.dot(slot_rows, gate_weight[0], preferred_element_type=jnp.float32)
    up_act = jnp.dot(slot_rows, up_weight[0], preferred_element_type=jnp.float32)
    hidden = (jax.nn.silu(gate_act) * up_act).astype(jnp.bfloat16)
    return jnp.dot(hidden, down_weight[0], preferred_element_type=jnp.float32)


def exchange_rows(residual_sum, normed, expert_ids, gate_values, gate_weight, up_weight, down_weight):
    model_width = normed.shape[1]
    row_total = normed.shape[0]
    top_count = expert_ids.shape[1]
    experts = lax.axis_size("ep")
    capacity = min(
        row_total, max(2, (5 * row_total * top_count + 4 * experts - 1) // (4 * experts))
    )
    chosen = expert_ids.reshape(-1)
    chosen_hot = (chosen[:, None] == jnp.arange(experts, dtype=jnp.int32)[None, :]).astype(
        jnp.int32
    )
    chosen_rank = jnp.sum(jnp.cumsum(chosen_hot, axis=0) * chosen_hot, axis=1) - 1
    slot_place = chosen * capacity + chosen_rank
    source_row = jnp.arange(row_total * top_count, dtype=jnp.int32) // top_count
    slot_source = jnp.zeros((experts * capacity,), jnp.int32).at[slot_place].set(source_row)
    slot_used = jnp.zeros((experts * capacity,), jnp.bool_).at[slot_place].set(True)
    outgoing = jnp.where(slot_used[:, None], normed[slot_source], jnp.zeros((), jnp.bfloat16))
    arrived = lax.all_to_all(outgoing, "ep", split_axis=0, concat_axis=0, tiled=True)
    partial_out = expert_terms(
        lax.all_gather(arrived, "ex", axis=0, tiled=True), gate_weight, up_weight, down_weight
    )
    summed = lax.psum_scatter(
        partial_out.astype(jnp.bfloat16), "ex", scatter_dimension=0, tiled=True
    )
    returned = lax.all_to_all(summed, "ep", split_axis=0, concat_axis=0, tiled=True)
    picked = returned[slot_place].reshape(row_total, top_count, model_width)
    mixture = jnp.einsum("rk,rkd->rd", gate_values, picked.astype(jnp.float32))
    return residual_sum + mixture


def normalise(rows, norm_gain):
    mean_square = jnp.mean(rows * rows, axis=1, keepdims=True)
    return (rows * lax.rsqrt(mean_square + eps) * norm_gain).astype(jnp.bfloat16)


def column_of(expert_ids, gate_values, experts):
    numbers = jnp.arange(experts, dtype=jnp.int32)
    return jnp.sum(
        jnp.where(expert_ids[:, :, None] == numbers, gate_values[:, :, None], 0.0), axis=1
    )


def layer_kernel(
    rows, normed, total, weight, gate_hbm, up_hbm, down_hbm, out,
    held, gate, up, down, hidden, core_in, diag_in, side_in, far_in,
    send_sem, recv_sem, load_sem,
):
    width = normed.shape[1]
    half = width // 2
    units = hidden.shape[1]
    me = lax.axis_index("ep")
    plane = me // 8
    local = me % 8
    sibling = me + 1 - 2 * (me % 2)
    x_peer = me + 2 - 4 * ((me // 2) % 2)
    y_peer = me + 4 - 8 * ((me // 4) % 2)
    z_peer = (
        me,
        (plane + 1 - 2 * (plane % 2)) * 8 + local,
        ((plane + 2) % 4) * 8 + local,
        (3 - plane) * 8 + local,
    )
    loads = [
        pltpu.make_async_copy(gate_hbm.at[0], gate, load_sem.at[0]),
        pltpu.make_async_copy(up_hbm.at[0], up, load_sem.at[1]),
        pltpu.make_async_copy(down_hbm.at[0], down, load_sem.at[2]),
    ]
    for load in loads:
        load.start()
    barrier = pltpu.get_barrier_semaphore()
    for peer in (sibling, x_peer, y_peer) + z_peer[1:]:
        pl.semaphore_signal(
            barrier, inc=1, device_id={"ep": peer}, device_id_type=pl.DeviceIdType.MESH
        )
    pl.semaphore_wait(barrier, 6)

    def remote(src, dst, k, slot, peer):
        return pltpu.make_async_remote_copy(
            src_ref=src,
            dst_ref=dst,
            send_sem=send_sem.at[k, slot],
            recv_sem=recv_sem.at[k, slot],
            device_id={"ep": peer},
            device_id_type=pl.DeviceIdType.MESH,
        )

    def block(k, b):
        return held.at[k, pl.ds(b * rows, rows), :]

    def side(k, b, low):
        return held.at[k, pl.ds(b * rows, rows), pl.ds(low, half)]

    ag_z = [
        remote(normed, block(k, 0), k, 0, z_peer[k]) if k else None for k in range(4)
    ]
    ag = []
    rs = []
    for k in range(4):
        ag.append(
            [
                remote(block(k, 0), block(k, 1), k, 1, x_peer),
                remote(block(k, 0), block(k, 2), k, 2, y_peer),
                remote(side(k, 1, 0), side(k, 3, 0), k, 3, y_peer),
                remote(side(k, 2, half), side(k, 3, half), k, 4, x_peer),
                remote(block(k, 0), block(k, 4), k, 5, sibling),
                remote(block(k, 1), block(k, 5), k, 6, sibling),
                remote(block(k, 2), block(k, 6), k, 7, sibling),
                remote(block(k, 3), block(k, 7), k, 8, sibling),
            ]
        )
        rs.append(
            [
                remote(held.at[k, pl.ds(4 * rows, 4 * rows), :], core_in.at[k], k, 9, sibling),
                remote(side(k, 3, 0), diag_in.at[k, 0], k, 10, y_peer),
                remote(side(k, 3, half), diag_in.at[k, 1], k, 11, x_peer),
                remote(block(k, 1), side_in.at[k, 0], k, 12, x_peer),
                remote(block(k, 2), side_in.at[k, 1], k, 13, y_peer),
                remote(block(k, 0), far_in.at[k - 1], k, 14, z_peer[k]) if k else None,
            ]
        )

    def a1(k):
        if k:
            ag_z[k].wait_recv()
        for i in (0, 1, 4):
            ag[k][i].start()

    def a2(k):
        ag[k][0].wait_recv()
        ag[k][2].start()
        ag[k][5].start()
        ag[k][1].wait_recv()
        ag[k][3].start()
        ag[k][6].start()

    def a3(k):
        ag[k][2].wait_recv()
        ag[k][3].wait_recv()
        ag[k][7].start()

    def a4(k):
        for i in range(4, 8):
            ag[k][i].wait_recv()

    def hidden_units(k):
        tile = units // 3

        @pl.loop(0, 3)
        def _(n):
            columns = pl.ds(pl.multiple_of(n * tile, tile), tile)
            gate_act = jnp.dot(held[k], gate[:, columns], preferred_element_type=jnp.float32)
            up_act = jnp.dot(held[k], up[:, columns], preferred_element_type=jnp.float32)
            act = gate_act / (1.0 + jnp.exp(-gate_act)) * up_act
            hidden[:, columns] = act.astype(jnp.bfloat16)

    def down_units(k, part):
        tile = 512
        count = width // tile // 2

        @pl.loop(part * count, (part + 1) * count)
        def _(n):
            columns = pl.ds(pl.multiple_of(n * tile, tile), tile)
            term = jnp.dot(hidden[...], down[:, columns], preferred_element_type=jnp.float32)
            held[k, :, columns] = (term * weight[k]).astype(jnp.bfloat16)

    def add_into(k, b, low, size, source):
        tile = 512

        @pl.loop(0, size // tile)
        def _(n):
            mine = pl.ds(pl.multiple_of(low + n * tile, tile), tile)
            theirs = pl.ds(pl.multiple_of(n * tile, tile), tile)
            spot = pl.ds(b * rows, rows)
            added = held[k, spot, mine].astype(jnp.float32)
            for ref in source:
                added = added + ref[:, theirs].astype(jnp.float32)
            held[k, spot, mine] = added.astype(jnp.bfloat16)

    def from_core(k, b):
        return core_in.at[k, pl.ds(b * rows, rows), :]

    def r1(k):
        rs[k][0].start()

    def r2(k):
        rs[k][0].wait_recv()
        add_into(k, 3, 0, width, [from_core(k, 3)])
        rs[k][1].start()
        rs[k][2].start()
        add_into(k, 1, half, half, [core_in.at[k, pl.ds(rows, rows), pl.ds(half, half)]])
        add_into(k, 2, 0, half, [core_in.at[k, pl.ds(2 * rows, rows), pl.ds(0, half)]])

    def r3(k):
        rs[k][1].wait_recv()
        add_into(
            k, 1, 0, half,
            [core_in.at[k, pl.ds(rows, rows), pl.ds(0, half)], diag_in.at[k, 0]],
        )
        rs[k][3].start()
        rs[k][2].wait_recv()
        add_into(
            k, 2, half, half,
            [core_in.at[k, pl.ds(2 * rows, rows), pl.ds(half, half)], diag_in.at[k, 1]],
        )
        rs[k][4].start()

    def r4(k):
        rs[k][3].wait_recv()
        rs[k][4].wait_recv()
        add_into(k, 0, 0, width, [from_core(k, 0), side_in.at[k, 0], side_in.at[k, 1]])
        if k:
            rs[k][5].start()

    def settle(k):
        for copy in ag[k]:
            copy.wait_send()

    for k in (1, 2, 3):
        ag_z[k].start()
    held[0, pl.ds(0, rows), :] = normed[...]
    a1(0)
    a2(0)
    a1(1)
    a3(0)
    a4(0)
    a2(1)
    loads[0].wait()
    loads[1].wait()
    loads[2].wait()
    hidden_units(0)
    settle(0)
    a3(1)
    a1(2)
    down_units(0, 0)
    a2(2)
    down_units(0, 1)
    r1(0)
    a4(1)
    a1(3)
    hidden_units(1)
    settle(1)
    a3(2)
    r2(0)
    a2(3)
    down_units(1, 0)
    r3(0)
    down_units(1, 1)
    r1(1)
    a4(2)
    hidden_units(2)
    settle(2)
    a3(3)
    r2(1)
    down_units(2, 0)
    r3(1)
    down_units(2, 1)
    r1(2)
    a4(3)
    r4(1)
    hidden_units(3)
    settle(3)
    r2(2)
    down_units(3, 0)
    r3(2)
    down_units(3, 1)
    r1(3)
    r4(2)
    r4(0)
    r2(3)
    r3(3)
    r4(3)
    for k in (1, 2, 3):
        rs[k][5].wait_recv()

    @pl.loop(0, width // 512)
    def _(n):
        columns = pl.ds(pl.multiple_of(n * 512, 512), 512)
        mixture = held[0, pl.ds(0, rows), columns].astype(jnp.float32)
        for k in range(3):
            mixture = mixture + far_in[k, :, columns].astype(jnp.float32)
        out[:, columns] = (total[:, columns] + mixture).astype(jnp.bfloat16)

    for k in range(4):
        if k:
            ag_z[k].wait_send()
        for copy in rs[k]:
            if copy is not None:
                copy.wait_send()


def fused_layer(residual_sum, normed, weight, gate_weight, up_weight, down_weight):
    rows, width = normed.shape
    units = gate_weight.shape[2]
    bf16 = jnp.bfloat16
    vmem = pl.BlockSpec(memory_space=pltpu.VMEM)
    anywhere = pl.BlockSpec(memory_space=pl.ANY)
    return pl.pallas_call(
        functools.partial(layer_kernel, rows),
        out_shape=jax.ShapeDtypeStruct((rows, width), bf16),
        in_specs=[vmem] * 3 + [anywhere] * 3,
        out_specs=vmem,
        scratch_shapes=[
            pltpu.VMEM((4, 8 * rows, width), bf16),
            pltpu.VMEM((width, units), bf16),
            pltpu.VMEM((width, units), bf16),
            pltpu.VMEM((units, width), bf16),
            pltpu.VMEM((8 * rows, units), bf16),
            pltpu.VMEM((4, 4 * rows, width), bf16),
            pltpu.VMEM((4, 2, rows, width // 2), bf16),
            pltpu.VMEM((4, 2, rows, width), bf16),
            pltpu.VMEM((3, rows, width), bf16),
            pltpu.SemaphoreType.DMA((4, 15)),
            pltpu.SemaphoreType.DMA((4, 15)),
            pltpu.SemaphoreType.DMA((3,)),
        ],
        compiler_params=pltpu.CompilerParams(
            collective_id=0, has_side_effects=True, vmem_limit_bytes=60 * 1024 * 1024
        ),
    )(normed, residual_sum, weight, gate_weight, up_weight, down_weight)


def send_order():
    block = jnp.arange(8, dtype=jnp.int32)
    flips = (block % 2) * 2 + (block // 2 % 2) * 4 + block // 4
    return (jnp.arange(4, dtype=jnp.int32)[:, None] * 8 + flips[None, :]).reshape(-1)


def on_device(
    residual,
    queries,
    new_kv,
    cache_pool,
    page_table,
    context_len,
    prefill_hidden,
    prefill_kv,
    prefill_dest,
    prefill_slot,
    expert_ids,
    gate_values,
    norm_gain,
    gate_weight,
    up_weight,
    down_weight,
):
    decode_rows = residual.shape[0]
    devices = lax.axis_size(("ep", "ex"))
    pre_rows = prefill_kv.shape[0]
    pages = page_table.reshape(decode_rows, -1)
    cache = cache_pool[pages].reshape(decode_rows, -1, cache_pool.shape[2])
    lengths = context_len.reshape(decode_rows)
    kv_slots = max(1, (5 * pre_rows + 4 * devices - 1) // (4 * devices))
    target = prefill_dest[:, 0]
    target_hot = (target[:, None] == jnp.arange(devices, dtype=jnp.int32)[None, :]).astype(
        jnp.int32
    )
    target_rank = jnp.sum(jnp.cumsum(target_hot, axis=0) * target_hot, axis=1) - 1
    target_place = target * kv_slots + target_rank
    send_kv = (
        jnp.zeros((devices * kv_slots, prefill_kv.shape[1]), jnp.bfloat16)
        .at[target_place]
        .set(prefill_kv)
    )
    send_slot = jnp.full((devices * kv_slots,), -1, jnp.int32).at[target_place].set(prefill_slot)
    fused = lax.axis_size("ex") == 1 and devices == 32 and lax.axis_size("parts") == 1
    if fused:
        columns = column_of(expert_ids, gate_values, devices).T
        high = lax.reduce_precision(columns, 8, 7)
        low = columns - high
        extra = jnp.concatenate(
            [high, low, send_slot.reshape(devices, kv_slots).astype(jnp.float32)], axis=1
        ).astype(jnp.bfloat16)
        spare = prefill_kv.shape[1] - extra.shape[1]
        payload = jnp.concatenate(
            [
                send_kv.reshape(devices, kv_slots, -1),
                jnp.pad(extra, ((0, 0), (0, spare)))[:, None, :],
            ],
            axis=1,
        )
        payload = lax.all_to_all(payload, ("ep", "ex"), split_axis=0, concat_axis=0, tiled=True)
        hand_kv = payload[:, :kv_slots].reshape(devices * kv_slots, -1)
        extra = payload[:, kv_slots].astype(jnp.float32)
        row_total = columns.shape[1]
        weight = extra[:, :row_total] + extra[:, row_total : 2 * row_total]
        hand_slot = extra[:, 2 * row_total : 2 * row_total + kv_slots].reshape(-1).astype(jnp.int32)
    else:
        hand_kv, hand_slot = (
            lax.all_to_all(send_kv, ("ep", "ex"), split_axis=0, concat_axis=0, tiled=True),
            lax.all_to_all(send_slot, ("ep", "ex"), split_axis=0, concat_axis=0, tiled=True),
        )
    hand_ok = hand_slot[None, :] == jnp.arange(decode_rows, dtype=jnp.int32)[:, None]
    attention = attend(queries, new_kv, cache, lengths, hand_kv, hand_ok)
    decode_sum = residual.astype(jnp.float32) + attention
    prefill_sum = prefill_hidden.astype(jnp.float32)
    weights = (gate_weight, up_weight, down_weight)
    residual_sum = jnp.concatenate([decode_sum, prefill_sum], axis=0)
    if fused:
        normed = normalise(residual_sum, norm_gain)
        order = lax.axis_index("ep") ^ send_order()
        weight = weight[order].reshape(4, -1, 1)
        result = fused_layer(residual_sum, normed, weight, *weights)
        return (result[:decode_rows], result[decode_rows:])
    result = exchange_rows(
        residual_sum,
        normalise(residual_sum, norm_gain),
        expert_ids,
        gate_values,
        *weights,
    ).astype(jnp.bfloat16)
    return (result[:decode_rows], result[decode_rows:])


def solution(mesh):
    in_specs = (
        P(("parts", "ep", "ex"), None),
        P(("parts", "ep", "ex"), None),
        P(("parts", "ep", "ex"), None),
        P(("parts", "ep", "ex"), None, None),
        P(("parts", "ep", "ex"), None),
        P(("parts", "ep", "ex"), None),
        P(("parts", "ep", "ex"), None),
        P(("parts", "ep", "ex"), None),
        P(("parts", "ep", "ex"), None),
        P(("parts", "ep", "ex")),
        P(("parts", "ep", "ex"), None),
        P(("parts", "ep", "ex"), None),
        P(),
        P("ep", None, "ex"),
        P("ep", None, "ex"),
        P("ep", "ex", None),
    )
    out_specs = (P(("parts", "ep", "ex"), None), P(("parts", "ep", "ex"), None))
    return jax.shard_map(
        on_device, mesh=mesh, in_specs=in_specs, out_specs=out_specs, check_vma=False
    )
```

```python
import functools

import jax
import jax.numpy as jnp
from jax import lax
from jax.experimental import pallas as pl
from jax.experimental.pallas import tpu as pltpu
from jax.sharding import PartitionSpec as P

HD = 128
KVH = 2


neg_big = -1e30
eps = 1e-06


def attend(queries, new_kv, cache, context_len, hand_kv, hand_ok):
    row_count = queries.shape[0]
    kv_width = new_kv.shape[1] // 2
    group_size = queries.shape[1] // kv_width
    positions = cache.shape[1]
    query_heads = queries.reshape(row_count, KVH, group_size, HD)
    cache_keys = cache[:, :, :kv_width].reshape(row_count, positions, KVH, HD)
    cache_values = cache[:, :, kv_width:].reshape(row_count, positions, KVH, HD)
    hand_keys = hand_kv[:, :kv_width].reshape(-1, KVH, HD)
    hand_values = hand_kv[:, kv_width:].reshape(-1, KVH, HD)
    own_keys = new_kv[:, :kv_width].reshape(row_count, KVH, HD)
    own_values = new_kv[:, kv_width:].reshape(row_count, KVH, HD)
    score_scale = HD ** (-0.5)
    cache_scores = (
        jnp.einsum("rgjd,rtgd->rgjt", query_heads, cache_keys, preferred_element_type=jnp.float32)
        * score_scale
    )
    live_mask = jnp.arange(positions, dtype=jnp.int32)[None, :] < context_len[:, None]
    cache_scores = jnp.where(live_mask[:, None, None, :], cache_scores, neg_big)
    hand_scores = (
        jnp.einsum("rgjd,mgd->rgjm", query_heads, hand_keys, preferred_element_type=jnp.float32)
        * score_scale
    )
    hand_scores = jnp.where(hand_ok[:, None, None, :], hand_scores, neg_big)
    own_scores = (
        jnp.einsum("rgjd,rgd->rgj", query_heads, own_keys, preferred_element_type=jnp.float32)
        * score_scale
    )
    largest = jnp.maximum(
        jnp.maximum(jnp.max(cache_scores, -1), jnp.max(hand_scores, -1)), own_scores
    )
    cache_exp = jnp.exp(cache_scores - largest[..., None])
    hand_exp = jnp.exp(hand_scores - largest[..., None])
    own_exp = jnp.exp(own_scores - largest)
    denominator = jnp.sum(cache_exp, -1) + jnp.sum(hand_exp, -1) + own_exp
    cache_probs = (cache_exp / denominator[..., None]).astype(jnp.bfloat16)
    hand_probs = (hand_exp / denominator[..., None]).astype(jnp.bfloat16)
    own_probs = (own_exp / denominator).astype(jnp.bfloat16)
    attended = jnp.einsum(
        "rgjt,rtgd->rgjd", cache_probs, cache_values, preferred_element_type=jnp.float32
    )
    attended = attended + jnp.einsum(
        "rgjm,mgd->rgjd", hand_probs, hand_values, preferred_element_type=jnp.float32
    )
    attended = (
        attended
        + own_probs.astype(jnp.float32)[..., None] * own_values.astype(jnp.float32)[:, :, None, :]
    )
    return attended.reshape(row_count, -1)


def expert_terms(slot_rows, gate_weight, up_weight, down_weight):
    gate_act = jnp.dot(slot_rows, gate_weight[0], preferred_element_type=jnp.float32)
    up_act = jnp.dot(slot_rows, up_weight[0], preferred_element_type=jnp.float32)
    hidden = (jax.nn.silu(gate_act) * up_act).astype(jnp.bfloat16)
    return jnp.dot(hidden, down_weight[0], preferred_element_type=jnp.float32)


def exchange_rows(residual_sum, normed, expert_ids, gate_values, gate_weight, up_weight, down_weight):
    model_width = normed.shape[1]
    row_total = normed.shape[0]
    top_count = expert_ids.shape[1]
    experts = lax.axis_size("ep")
    capacity = min(
        row_total, max(2, (5 * row_total * top_count + 4 * experts - 1) // (4 * experts))
    )
    chosen = expert_ids.reshape(-1)
    chosen_hot = (chosen[:, None] == jnp.arange(experts, dtype=jnp.int32)[None, :]).astype(
        jnp.int32
    )
    chosen_rank = jnp.sum(jnp.cumsum(chosen_hot, axis=0) * chosen_hot, axis=1) - 1
    slot_place = chosen * capacity + chosen_rank
    source_row = jnp.arange(row_total * top_count, dtype=jnp.int32) // top_count
    slot_source = jnp.zeros((experts * capacity,), jnp.int32).at[slot_place].set(source_row)
    slot_used = jnp.zeros((experts * capacity,), jnp.bool_).at[slot_place].set(True)
    outgoing = jnp.where(slot_used[:, None], normed[slot_source], jnp.zeros((), jnp.bfloat16))
    arrived = lax.all_to_all(outgoing, "ep", split_axis=0, concat_axis=0, tiled=True)
    partial_out = expert_terms(
        lax.all_gather(arrived, "ex", axis=0, tiled=True), gate_weight, up_weight, down_weight
    )
    summed = lax.psum_scatter(
        partial_out.astype(jnp.bfloat16), "ex", scatter_dimension=0, tiled=True
    )
    returned = lax.all_to_all(summed, "ep", split_axis=0, concat_axis=0, tiled=True)
    picked = returned[slot_place].reshape(row_total, top_count, model_width)
    mixture = jnp.einsum("rk,rkd->rd", gate_values, picked.astype(jnp.float32))
    return residual_sum + mixture


def normalise(rows, norm_gain):
    mean_square = jnp.mean(rows * rows, axis=1, keepdims=True)
    return (rows * lax.rsqrt(mean_square + eps) * norm_gain).astype(jnp.bfloat16)


def column_of(expert_ids, gate_values, experts):
    numbers = jnp.arange(experts, dtype=jnp.int32)
    return jnp.sum(
        jnp.where(expert_ids[:, :, None] == numbers, gate_values[:, :, None], 0.0), axis=1
    )


def layer_kernel(
    rows, normed, total, weight, gate_hbm, up_hbm, down_hbm, out,
    held, gate, up, down, hidden, core_in, diag_in, side_in, far_in,
    send_sem, recv_sem, load_sem,
):
    width = normed.shape[1]
    half = width // 2
    units = hidden.shape[1]
    me = lax.axis_index("ep")
    plane = me // 8
    local = me % 8
    sibling = me + 1 - 2 * (me % 2)
    x_peer = me + 2 - 4 * ((me // 2) % 2)
    y_peer = me + 4 - 8 * ((me // 4) % 2)
    z_peer = (
        me,
        (plane + 1 - 2 * (plane % 2)) * 8 + local,
        ((plane + 2) % 4) * 8 + local,
        (3 - plane) * 8 + local,
    )
    loads = [
        pltpu.make_async_copy(gate_hbm.at[0], gate, load_sem.at[0]),
        pltpu.make_async_copy(up_hbm.at[0], up, load_sem.at[1]),
        pltpu.make_async_copy(down_hbm.at[0], down, load_sem.at[2]),
    ]
    for load in loads:
        load.start()
    barrier = pltpu.get_barrier_semaphore()
    for peer in (sibling, x_peer, y_peer) + z_peer[1:]:
        pl.semaphore_signal(
            barrier, inc=1, device_id={"ep": peer}, device_id_type=pl.DeviceIdType.MESH
        )
    pl.semaphore_wait(barrier, 6)

    def remote(src, dst, k, slot, peer):
        return pltpu.make_async_remote_copy(
            src_ref=src,
            dst_ref=dst,
            send_sem=send_sem.at[k, slot],
            recv_sem=recv_sem.at[k, slot],
            device_id={"ep": peer},
            device_id_type=pl.DeviceIdType.MESH,
        )

    def block(k, b):
        return held.at[k, pl.ds(b * rows, rows), :]

    def side(k, b, low):
        return held.at[k, pl.ds(b * rows, rows), pl.ds(low, half)]

    ag_z = [
        remote(normed, block(k, 0), k, 0, z_peer[k]) if k else None for k in range(4)
    ]
    ag = []
    rs = []
    for k in range(4):
        ag.append(
            [
                remote(block(k, 0), block(k, 1), k, 1, x_peer),
                remote(block(k, 0), block(k, 2), k, 2, y_peer),
                remote(side(k, 1, 0), side(k, 3, 0), k, 3, y_peer),
                remote(side(k, 2, half), side(k, 3, half), k, 4, x_peer),
                remote(block(k, 0), block(k, 4), k, 5, sibling),
                remote(block(k, 1), block(k, 5), k, 6, sibling),
                remote(block(k, 2), block(k, 6), k, 7, sibling),
                remote(block(k, 3), block(k, 7), k, 8, sibling),
            ]
        )
        rs.append(
            [
                remote(held.at[k, pl.ds(4 * rows, 4 * rows), :], core_in.at[k], k, 9, sibling),
                remote(side(k, 3, 0), diag_in.at[k, 0], k, 10, y_peer),
                remote(side(k, 3, half), diag_in.at[k, 1], k, 11, x_peer),
                remote(block(k, 1), side_in.at[k, 0], k, 12, x_peer),
                remote(block(k, 2), side_in.at[k, 1], k, 13, y_peer),
                remote(block(k, 0), far_in.at[k - 1], k, 14, z_peer[k]) if k else None,
            ]
        )

    def a1(k):
        if k:
            ag_z[k].wait_recv()
        for i in (0, 1, 4):
            ag[k][i].start()

    def a2(k):
        ag[k][0].wait_recv()
        ag[k][2].start()
        ag[k][5].start()
        ag[k][1].wait_recv()
        ag[k][3].start()
        ag[k][6].start()

    def a3(k):
        ag[k][2].wait_recv()
        ag[k][3].wait_recv()
        ag[k][7].start()

    def a4(k):
        for i in range(4, 8):
            ag[k][i].wait_recv()

    def hidden_units(k, n):
        tile = units // 3
        columns = pl.ds(n * tile, tile)
        gate_act = jnp.dot(held[k], gate[:, columns], preferred_element_type=jnp.float32)
        up_act = jnp.dot(held[k], up[:, columns], preferred_element_type=jnp.float32)
        act = gate_act / (1.0 + jnp.exp(-gate_act)) * up_act
        hidden[:, columns] = act.astype(jnp.bfloat16)

    def down_units(k, part):
        tile = 512
        count = width // tile // 2

        @pl.loop(part * count, (part + 1) * count)
        def _(n):
            columns = pl.ds(pl.multiple_of(n * tile, tile), tile)
            term = jnp.dot(hidden[...], down[:, columns], preferred_element_type=jnp.float32)
            held[k, :, columns] = (term * weight[k]).astype(jnp.bfloat16)

    def add_into(k, b, low, size, source):
        tile = 512

        @pl.loop(0, size // tile)
        def _(n):
            mine = pl.ds(pl.multiple_of(low + n * tile, tile), tile)
            theirs = pl.ds(pl.multiple_of(n * tile, tile), tile)
            spot = pl.ds(b * rows, rows)
            added = held[k, spot, mine].astype(jnp.float32)
            for ref in source:
                added = added + ref[:, theirs].astype(jnp.float32)
            held[k, spot, mine] = added.astype(jnp.bfloat16)

    def from_core(k, b):
        return core_in.at[k, pl.ds(b * rows, rows), :]

    def r1(k):
        rs[k][0].start()

    def r2(k):
        rs[k][0].wait_recv()
        add_into(k, 3, 0, width, [from_core(k, 3)])
        rs[k][1].start()
        rs[k][2].start()
        add_into(k, 1, half, half, [core_in.at[k, pl.ds(rows, rows), pl.ds(half, half)]])
        add_into(k, 2, 0, half, [core_in.at[k, pl.ds(2 * rows, rows), pl.ds(0, half)]])

    def r3(k):
        rs[k][1].wait_recv()
        add_into(
            k, 1, 0, half,
            [core_in.at[k, pl.ds(rows, rows), pl.ds(0, half)], diag_in.at[k, 0]],
        )
        rs[k][3].start()
        rs[k][2].wait_recv()
        add_into(
            k, 2, half, half,
            [core_in.at[k, pl.ds(2 * rows, rows), pl.ds(half, half)], diag_in.at[k, 1]],
        )
        rs[k][4].start()

    def r4(k):
        rs[k][3].wait_recv()
        rs[k][4].wait_recv()
        add_into(k, 0, 0, width, [from_core(k, 0), side_in.at[k, 0], side_in.at[k, 1]])
        if k:
            rs[k][5].start()

    def settle(k):
        for copy in ag[k]:
            copy.wait_send()

    inner = jnp.logical_or(plane == 1, plane == 2)
    ag_z[1].start()

    @pl.when(inner)
    def _():
        ag_z[3].start()

    held[0, pl.ds(0, rows), :] = normed[...]
    a1(0)
    loads[0].wait()
    loads[1].wait()
    loads[2].wait()
    ag_z[1].wait_send()
    ag_z[2].start()
    a1(1)
    a2(0)
    a3(0)
    a4(0)
    hidden_units(0, 0)
    a2(1)
    hidden_units(0, 1)
    a3(1)
    hidden_units(0, 2)
    settle(0)
    ag_z[2].wait_send()

    @pl.when(jnp.logical_not(inner))
    def _():
        ag_z[3].start()

    a1(2)
    down_units(0, 0)
    down_units(0, 1)
    r1(0)
    a4(1)
    hidden_units(1, 0)
    a2(2)
    hidden_units(1, 1)
    a1(3)
    hidden_units(1, 2)
    settle(1)
    a3(2)
    down_units(1, 0)
    down_units(1, 1)
    r1(1)
    r2(1)
    a2(3)
    a4(2)
    hidden_units(2, 0)
    r3(1)
    hidden_units(2, 1)
    a3(3)
    hidden_units(2, 2)
    settle(2)
    down_units(2, 0)
    down_units(2, 1)
    r1(2)
    r2(2)
    r4(1)
    a4(3)
    hidden_units(3, 0)
    r3(2)
    hidden_units(3, 1)
    hidden_units(3, 2)
    settle(3)
    down_units(3, 0)
    down_units(3, 1)
    r1(3)
    r2(3)
    r4(2)
    r2(0)
    r3(3)
    r3(0)
    r4(3)
    r4(0)
    for k in (1, 2, 3):
        rs[k][5].wait_recv()

    @pl.loop(0, width // 512)
    def _(n):
        columns = pl.ds(pl.multiple_of(n * 512, 512), 512)
        mixture = held[0, pl.ds(0, rows), columns].astype(jnp.float32)
        for k in range(3):
            mixture = mixture + far_in[k, :, columns].astype(jnp.float32)
        out[:, columns] = (total[:, columns] + mixture).astype(jnp.bfloat16)

    for k in range(4):
        if k == 3:
            ag_z[k].wait_send()
        for copy in rs[k]:
            if copy is not None:
                copy.wait_send()


def fused_layer(residual_sum, normed, weight, gate_weight, up_weight, down_weight):
    rows, width = normed.shape
    units = gate_weight.shape[2]
    bf16 = jnp.bfloat16
    vmem = pl.BlockSpec(memory_space=pltpu.VMEM)
    anywhere = pl.BlockSpec(memory_space=pl.ANY)
    return pl.pallas_call(
        functools.partial(layer_kernel, rows),
        out_shape=jax.ShapeDtypeStruct((rows, width), bf16),
        in_specs=[vmem] * 3 + [anywhere] * 3,
        out_specs=vmem,
        scratch_shapes=[
            pltpu.VMEM((4, 8 * rows, width), bf16),
            pltpu.VMEM((width, units), bf16),
            pltpu.VMEM((width, units), bf16),
            pltpu.VMEM((units, width), bf16),
            pltpu.VMEM((8 * rows, units), bf16),
            pltpu.VMEM((4, 4 * rows, width), bf16),
            pltpu.VMEM((4, 2, rows, width // 2), bf16),
            pltpu.VMEM((4, 2, rows, width), bf16),
            pltpu.VMEM((3, rows, width), bf16),
            pltpu.SemaphoreType.DMA((4, 15)),
            pltpu.SemaphoreType.DMA((4, 15)),
            pltpu.SemaphoreType.DMA((3,)),
        ],
        compiler_params=pltpu.CompilerParams(
            collective_id=0, has_side_effects=True, vmem_limit_bytes=60 * 1024 * 1024
        ),
    )(normed, residual_sum, weight, gate_weight, up_weight, down_weight)


def send_order():
    block = jnp.arange(8, dtype=jnp.int32)
    flips = (block % 2) * 2 + (block // 2 % 2) * 4 + block // 4
    return (jnp.arange(4, dtype=jnp.int32)[:, None] * 8 + flips[None, :]).reshape(-1)


def on_device(
    residual,
    queries,
    new_kv,
    cache_pool,
    page_table,
    context_len,
    prefill_hidden,
    prefill_kv,
    prefill_dest,
    prefill_slot,
    expert_ids,
    gate_values,
    norm_gain,
    gate_weight,
    up_weight,
    down_weight,
):
    decode_rows = residual.shape[0]
    devices = lax.axis_size(("ep", "ex"))
    pre_rows = prefill_kv.shape[0]
    pages = page_table.reshape(decode_rows, -1)
    cache = cache_pool[pages].reshape(decode_rows, -1, cache_pool.shape[2])
    lengths = context_len.reshape(decode_rows)
    kv_slots = max(1, (5 * pre_rows + 4 * devices - 1) // (4 * devices))
    target = prefill_dest[:, 0]
    target_hot = (target[:, None] == jnp.arange(devices, dtype=jnp.int32)[None, :]).astype(
        jnp.int32
    )
    target_rank = jnp.sum(jnp.cumsum(target_hot, axis=0) * target_hot, axis=1) - 1
    target_place = target * kv_slots + target_rank
    send_kv = (
        jnp.zeros((devices * kv_slots, prefill_kv.shape[1]), jnp.bfloat16)
        .at[target_place]
        .set(prefill_kv)
    )
    send_slot = jnp.full((devices * kv_slots,), -1, jnp.int32).at[target_place].set(prefill_slot)
    fused = lax.axis_size("ex") == 1 and devices == 32 and lax.axis_size("parts") == 1
    if fused:
        columns = column_of(expert_ids, gate_values, devices).T
        high = lax.reduce_precision(columns, 8, 7)
        low = columns - high
        extra = jnp.concatenate(
            [high, low, send_slot.reshape(devices, kv_slots).astype(jnp.float32)], axis=1
        ).astype(jnp.bfloat16)
        spare = prefill_kv.shape[1] - extra.shape[1]
        payload = jnp.concatenate(
            [
                send_kv.reshape(devices, kv_slots, -1),
                jnp.pad(extra, ((0, 0), (0, spare)))[:, None, :],
            ],
            axis=1,
        )
        payload = lax.all_to_all(payload, ("ep", "ex"), split_axis=0, concat_axis=0, tiled=True)
        hand_kv = payload[:, :kv_slots].reshape(devices * kv_slots, -1)
        extra = payload[:, kv_slots].astype(jnp.float32)
        row_total = columns.shape[1]
        weight = extra[:, :row_total] + extra[:, row_total : 2 * row_total]
        hand_slot = extra[:, 2 * row_total : 2 * row_total + kv_slots].reshape(-1).astype(jnp.int32)
    else:
        hand_kv, hand_slot = (
            lax.all_to_all(send_kv, ("ep", "ex"), split_axis=0, concat_axis=0, tiled=True),
            lax.all_to_all(send_slot, ("ep", "ex"), split_axis=0, concat_axis=0, tiled=True),
        )
    hand_ok = hand_slot[None, :] == jnp.arange(decode_rows, dtype=jnp.int32)[:, None]
    attention = attend(queries, new_kv, cache, lengths, hand_kv, hand_ok)
    decode_sum = residual.astype(jnp.float32) + attention
    prefill_sum = prefill_hidden.astype(jnp.float32)
    weights = (gate_weight, up_weight, down_weight)
    residual_sum = jnp.concatenate([decode_sum, prefill_sum], axis=0)
    if fused:
        normed = normalise(residual_sum, norm_gain)
        order = lax.axis_index("ep") ^ send_order()
        weight = weight[order].reshape(4, -1, 1)
        result = fused_layer(residual_sum, normed, weight, *weights)
        return (result[:decode_rows], result[decode_rows:])
    result = exchange_rows(
        residual_sum,
        normalise(residual_sum, norm_gain),
        expert_ids,
        gate_values,
        *weights,
    ).astype(jnp.bfloat16)
    return (result[:decode_rows], result[decode_rows:])


def solution(mesh):
    in_specs = (
        P(("parts", "ep", "ex"), None),
        P(("parts", "ep", "ex"), None),
        P(("parts", "ep", "ex"), None),
        P(("parts", "ep", "ex"), None, None),
        P(("parts", "ep", "ex"), None),
        P(("parts", "ep", "ex"), None),
        P(("parts", "ep", "ex"), None),
        P(("parts", "ep", "ex"), None),
        P(("parts", "ep", "ex"), None),
        P(("parts", "ep", "ex")),
        P(("parts", "ep", "ex"), None),
        P(("parts", "ep", "ex"), None),
        P(),
        P("ep", None, "ex"),
        P("ep", None, "ex"),
        P("ep", "ex", None),
    )
    out_specs = (P(("parts", "ep", "ex"), None), P(("parts", "ep", "ex"), None))
    return jax.shard_map(
        on_device, mesh=mesh, in_specs=in_specs, out_specs=out_specs, check_vma=False
    )
```
